32 devices in a mesh: parts: 2 (over y), row: 8 (over z, x), col: 2 (over core).
Axes of the slice: x: 2, y: 2, z: 4, core: 2. Of those that a mesh axis runs over, the one named last changes fastest.
Arguments:
- right_sides: float32 [16384, 2048], P(('parts', 'row'), 'col'), parts along dimension 0, may hold values from -6 to 6
- lower_panel: float32 [16384, 1024], P(('parts', 'row')), parts along dimension 0, as said below
- upper_panel: float32 [16384, 1024], P(('parts', 'row')), parts along dimension 0, as said below
Outputs:
- solution: float32 [16384, 2048], P(('parts', 'row'), 'col'), parts along dimension 0
The draws below stay inside these ranges and needn't reach their ends.
There are 2 independent parts, one for each index of `parts`. The reference program is written for one: setup_inputs(seed, part) draws one part's arguments, and reference() takes and returns one part's arrays. A program takes and returns all parts, laid end to end along the dimension named above; each array names one. Nothing has to cross between parts.
Inputs may be any that keep to these rules, and one draw needn't show every extreme that they name: `lower_panel`: column block k (columns k*256 to (k+1)*256 - 1) is zero in rows above k*256; its rows k*256 to (k+1)*256 - 1 form a unit lower triangular block. `upper_panel`: with b = 28 + j, column block j is zero in rows from (b+1)*256 on; its rows b*256 to (b+1)*256 - 1 form an upper triangular block whose diagonal entries have magnitudes from 1 to 2.
All inputs are finite; a program needn't handle non-finite values.
Results may differ from the reference program's by a relative error of at most 0.00013.
Values sent between devices are 32-bit elements; how exact they have to be, the bound alone decides.
A program may use at most 128 MiB of HBM per device.

```python
import jax
import jax.numpy as jnp
from jax import lax

NB = 256
KB = 4
R = 2048
M = 8192


def base_entries(key):
    entries = jnp.clip(jax.random.normal(key, (M, KB * NB), jnp.float32), -4.0, 4.0)
    row_scale = jax.random.uniform(jax.random.fold_in(key, 11), (M, 1), jnp.float32, minval=0.3, maxval=3.0)
    return (entries, row_scale)


def draw_lower_panel(key, part):
    entries, row_scale = base_entries(jax.random.fold_in(key, 3))
    rows = jnp.arange(M, dtype=jnp.int32)[:, None]
    columns = jnp.arange(KB * NB, dtype=jnp.int32)[None, :]
    first_row = columns // NB * NB
    offsets = rows - first_row
    inside = (rows >= first_row) & (rows < first_row + NB)
    below = rows >= first_row + NB
    strict = inside & (offsets > columns - first_row)
    unit = inside & (offsets == columns - first_row)
    scale = 1.0 / NB ** 0.5
    values = jnp.where(below, entries * row_scale * scale, 0.0)
    values = values + jnp.where(strict, entries * 0.3 * scale, 0.0)
    values = values + jnp.where(unit, 1.0, 0.0)
    return values.astype(jnp.float32)


def draw_upper_panel(key, part):
    entries, row_scale = base_entries(jax.random.fold_in(key, 5))
    rows = jnp.arange(M, dtype=jnp.int32)[:, None]
    columns = jnp.arange(KB * NB, dtype=jnp.int32)[None, :]
    first_row = (M // NB - KB + columns // NB) * NB
    local_column = columns % NB
    offsets = rows - first_row
    inside = (rows >= first_row) & (rows < first_row + NB)
    above = rows < first_row
    strict = inside & (offsets < local_column)
    on_diagonal = inside & (offsets == local_column)
    magnitude = jax.random.uniform(jax.random.fold_in(key, 7), (M, KB * NB), jnp.float32, minval=1.0, maxval=2.0)
    signs = jnp.where(jax.random.bernoulli(jax.random.fold_in(key, 9), 0.5, (M, KB * NB)), 1.0, -1.0)
    scale = 1.0 / NB ** 0.5
    values = jnp.where(above, entries * row_scale * scale, 0.0)
    values = values + jnp.where(strict, entries * 0.3 * scale, 0.0)
    values = values + jnp.where(on_diagonal, magnitude * signs, 0.0)
    return values.astype(jnp.float32)


def steps_of(key, dims, split, smallest, top_value):
    level = 1.0
    for position, blocks in split:
        heights = jax.random.uniform(jax.random.fold_in(jax.random.fold_in(key, 6), position), (blocks,), jnp.float32, smallest / len(split), top_value / len(split))
        level = level * jnp.repeat(jnp.exp(heights), dims[position] // blocks).reshape((-1,) + (1,) * (len(dims) - 1 - position))
    return level


def normal_values(key, shape, width, most, cuts=(), kind=jnp.bfloat16):
    gain = steps_of(key, shape, cuts, -0.22, 0.18) if cuts else 1.0
    drawn = jax.random.normal(key, shape, jnp.float32) * width * gain
    return jnp.minimum(jnp.maximum(drawn, -most), most).astype(kind)


def setup_inputs(seed: int = 0, part: int = 0) -> dict:
    arg_keys = jax.random.split(jax.random.key(seed), 4)
    part_splits = jax.random.split(jax.random.fold_in(arg_keys[3], part), 4)
    right_sides = normal_values(part_splits[0], (M, R), 1.0, 6.0, ((0, 8), (1, 2)), jnp.float32)
    lower_panel = draw_lower_panel(jax.random.fold_in(jax.random.fold_in(arg_keys[3], part), 71), part)
    upper_panel = draw_upper_panel(jax.random.fold_in(jax.random.fold_in(arg_keys[3], part), 71), part)
    return dict(right_sides=right_sides, lower_panel=lower_panel, upper_panel=upper_panel)


def reference(right_sides, lower_panel, upper_panel):
    precise = lax.Precision.HIGHEST
    current = right_sides.astype(jnp.float32)
    for column in range(KB):
        first_row = column * NB
        diagonal_block = lower_panel[first_row:first_row + NB, column * NB:(column + 1) * NB]
        solved = jax.scipy.linalg.solve_triangular(diagonal_block, current[first_row:first_row + NB], lower=True, unit_diagonal=True)
        below = lower_panel[first_row + NB:, column * NB:(column + 1) * NB]
        current = current.at[first_row + NB:].add(-jnp.dot(below, solved, precision=precise))
        current = current.at[first_row:first_row + NB].set(solved)
    total_blocks = M // NB
    for column in range(KB - 1, -1, -1):
        block_index = total_blocks - KB + column
        first_row = block_index * NB
        diagonal_block = upper_panel[first_row:first_row + NB, column * NB:(column + 1) * NB]
        solved = jax.scipy.linalg.solve_triangular(diagonal_block, current[first_row:first_row + NB], lower=False)
        above = upper_panel[:first_row, column * NB:(column + 1) * NB]
        current = current.at[:first_row].add(-jnp.dot(above, solved, precision=precise))
        current = current.at[first_row:first_row + NB].set(solved)
    return current
```

```python
import functools

import jax
import jax.numpy as jnp
from jax import lax
from jax.experimental import pallas as pl
from jax.experimental.pallas import tpu as pltpu
from jax.sharding import PartitionSpec as P

NB = 256
KB = 4
CW = 256
HALF = NB // 2
LAG = 8


def split(value):
    high = value.astype(jnp.bfloat16)
    low = (value - high.astype(jnp.float32)).astype(jnp.bfloat16)
    return high, low


def mm(a, b):
    return jnp.dot(a, b, preferred_element_type=jnp.float32)


def dot_split(a, b):
    return mm(a[0], b[0]) + (mm(a[0], b[1]) + mm(a[1], b[0]))


def dot3(a, b):
    return dot_split(split(a), split(b))


def triangular_inverses(matrices):
    rows = lax.broadcasted_iota(jnp.int32, (NB, NB), 0)
    columns = lax.broadcasted_iota(jnp.int32, (NB, NB), 1)
    same = rows == columns
    ident = jnp.where(same, 1.0, 0.0).astype(jnp.float32)
    scales, offs = [], []
    for matrix in matrices:
        diagonal = jnp.where(same, matrix, 0.0)
        by_row = 1.0 / jnp.sum(diagonal, axis=1, keepdims=True)
        scales.append(1.0 / jnp.sum(diagonal, axis=0, keepdims=True))
        offs.append(jnp.where(same, 0.0, matrix) * by_row)
    count = range(len(matrices))
    inner = (rows // 16) == (columns // 16)
    powers = [jnp.where(inner, -offs[i], 0.0) for i in count]
    results = [ident + powers[i] for i in count]
    reach = 2
    while reach < 16:
        powers = [dot3(powers[i], powers[i]) for i in count]
        results = [results[i] + dot3(results[i], powers[i]) for i in count]
        reach *= 2
    size = 16
    while size < NB:
        pair = ((rows // (2 * size)) == (columns // (2 * size))) & (
            (rows // size) != (columns // size)
        )
        halves = [split(results[i]) for i in count]
        middle = [
            dot_split(split(jnp.where(pair, offs[i], 0.0)), halves[i]) for i in count
        ]
        results = [results[i] - dot_split(halves[i], split(middle[i])) for i in count]
        size *= 2
    return [results[i] * scales[i] for i in count]


def kernel(
    nx, nz, b_ref, l_ref, u_ref, out_ref,
    acc, xbuf, zbuf, lf, uf, lhi, llo, uhi, ulo, diag, inv_hi, inv_lo,
    b_sem, l_sem, u_sem, d_sem, o_sem, recv_f, recv_b, send_f, send_b,
):
    rows = b_ref.shape[0]
    chunks = b_ref.shape[1] // CW
    blocks = chunks * KB
    n = nx * nz
    me = lax.axis_index("row")
    x = me % nx
    z = me // nx
    is_first = me == 0
    is_last = me == n - 1

    def load_b(c):
        return pltpu.make_async_copy(b_ref.at[:, pl.ds(c * CW, CW)], acc.at[c], b_sem.at[c])

    def load_l(k):
        return pltpu.make_async_copy(l_ref.at[:, pl.ds(k * NB, NB)], lf.at[k], l_sem.at[k])

    def load_u(k):
        return pltpu.make_async_copy(u_ref.at[:, pl.ds(k * NB, NB)], uf.at[k], u_sem.at[k])

    def load_d(source, k):
        return pltpu.make_async_copy(
            source.at[pl.ds(k * NB, NB), pl.ds(k * NB, NB)], diag.at[k], d_sem.at[k]
        )

    def store_out(c):
        return pltpu.make_async_copy(acc.at[c], out_ref.at[:, pl.ds(c * CW, CW)], o_sem.at[c])

    @pl.when(is_first)
    def _():
        for k in range(KB):
            load_d(l_ref, k).start()

    @pl.when(is_last)
    def _():
        for k in range(KB):
            load_d(u_ref, k).start()

    load_b(0).start()
    for k in range(KB):
        load_l(k).start()
    for c in range(1, chunks):
        load_b(c).start()
    for k in range(KB):
        load_u(k).start()

    barrier = pltpu.get_barrier_semaphore()
    neighbours = (
        (x >= 1, me - 1),
        (x < nx - 1, me + 1),
        (z >= 1, me - nx),
        (z < nz - 1, me + nx),
    )
    for there, other in neighbours:
        @pl.when(there)
        def _():
            pl.semaphore_signal(
                barrier, inc=1, device_id={"row": other},
                device_id_type=pl.DeviceIdType.MESH,
            )
    peers = sum(jnp.where(there, 1, 0) for there, _ in neighbours)
    pl.semaphore_wait(barrier, peers)

    @pl.when(is_first | is_last)
    def _():
        for k in range(KB):
            load_d(l_ref, k).wait()
        inverses = triangular_inverses([diag[k] for k in range(KB)])
        for k in range(KB):
            high, low = split(inverses[k])
            inv_hi[k] = high
            inv_lo[k] = low

    def children(px, pz, step):
        along_x, along_z = step, step * nx
        tree_a = (
            ((px == 0) & (pz < nz - 1), me + along_z),
            ((pz >= 1) & (px < nx - 1), me + along_x),
            ((pz == 1) & (px >= 1), me - along_z),
        )
        tree_b = (
            ((pz == 0) & (px < nx - 1), me + along_x),
            ((px >= 1) & (pz < nz - 1), me + along_z),
            ((px == 1) & (pz >= 1), me - along_x),
        )
        return (tree_a, tree_b)

    forward_children = children(x, z, 1)
    backward_children = children(nx - 1 - x, nz - 1 - z, -1)

    def remote(buf, recv, send, block, tree, child, other):
        piece = buf.at[block, pl.ds(tree * HALF, HALF), :]
        return pltpu.make_async_remote_copy(
            src_ref=piece, dst_ref=piece,
            send_sem=send.at[block, tree * 3 + child],
            recv_sem=recv.at[block, tree],
            device_id={"row": other}, device_id_type=pl.DeviceIdType.MESH,
        )

    def pass_on(buf, recv, send, block, tree, kids):
        for child in range(3):
            there, other = kids[tree][child]

            @pl.when(there)
            def _():
                remote(buf, recv, send, block, tree, child, other).start()

    def sent(buf, recv, send, block, kids):
        for tree in range(2):
            for child in range(3):
                there, other = kids[tree][child]

                @pl.when(there)
                def _():
                    remote(buf, recv, send, block, tree, child, other).wait_send()

    def sweep_step(block, c, k, owner, buf, recv, send, kids, early, full, high, low, wait_panel):
        @pl.when(owner)
        def _():
            target = acc[c, pl.ds(pl.multiple_of(k * NB, NB), NB), :]
            buf[block] = dot_split((inv_hi[k], inv_lo[k]), split(target))
            for tree in range(2):
                pass_on(buf, recv, send, block, tree, kids)

        @pl.when(jnp.logical_not(owner))
        def _():
            for tree in range(2):
                remote(buf, recv, send, block, tree, 0, me).wait_recv()
                pass_on(buf, recv, send, block, tree, kids)

        @pl.when(early)
        def _():
            wait_panel(k)
            first, second = split(full[k])
            high[k] = first
            low[k] = second

        acc[c] = acc[c] - dot_split((high[k], low[k]), split(buf[block]))

        @pl.when(owner)
        def _():
            acc[c, pl.ds(pl.multiple_of(k * NB, NB), NB), :] = buf[block]

    def event(e, carry):
        @pl.when(e < blocks)
        def _():
            c = e // KB
            k = e % KB

            @pl.when(k == 0)
            def _():
                load_b(c).wait()

            sweep_step(
                e, c, k, is_first, xbuf, recv_f, send_f, forward_children,
                e < KB, lf, lhi, llo, lambda k: load_l(k).wait(),
            )

        @pl.when(e >= LAG)
        def _():
            j = e - LAG
            c = j // KB
            k = KB - 1 - j % KB
            sweep_step(
                j, c, k, is_last, zbuf, recv_b, send_b, backward_children,
                j < KB, uf, uhi, ulo, lambda k: load_u(k).wait(),
            )

            @pl.when(k == 0)
            def _():
                store_out(c).start()

        return carry

    lax.fori_loop(0, blocks + LAG, event, 0)

    def finish(block, carry):
        sent(xbuf, recv_f, send_f, block, forward_children)
        sent(zbuf, recv_b, send_b, block, backward_children)
        return carry

    lax.fori_loop(0, blocks, finish, 0)
    for c in range(chunks):
        store_out(c).wait()


def grid_of(n):
    nx = 2 if n < 32 else 4
    return nx, n // nx


def shards(right_sides, lower_panel, upper_panel):
    rows, width = right_sides.shape
    nx, nz = grid_of(lax.axis_size("row"))
    chunks = width // CW
    blocks = chunks * KB
    f32, bf16 = jnp.float32, jnp.bfloat16
    return pl.pallas_call(
        functools.partial(kernel, nx, nz),
        out_shape=jax.ShapeDtypeStruct((rows, width), f32),
        in_specs=[pl.BlockSpec(memory_space=pl.ANY)] * 3,
        out_specs=pl.BlockSpec(memory_space=pl.ANY),
        scratch_shapes=[
            pltpu.VMEM((chunks, rows, CW), f32),
            pltpu.VMEM((blocks, NB, CW), f32),
            pltpu.VMEM((blocks, NB, CW), f32),
            pltpu.VMEM((KB, rows, NB), f32),
            pltpu.VMEM((KB, rows, NB), f32),
            pltpu.VMEM((KB, rows, NB), bf16),
            pltpu.VMEM((KB, rows, NB), bf16),
            pltpu.VMEM((KB, rows, NB), bf16),
            pltpu.VMEM((KB, rows, NB), bf16),
            pltpu.VMEM((KB, NB, NB), f32),
            pltpu.VMEM((KB, NB, NB), bf16),
            pltpu.VMEM((KB, NB, NB), bf16),
            pltpu.SemaphoreType.DMA((chunks,)),
            pltpu.SemaphoreType.DMA((KB,)),
            pltpu.SemaphoreType.DMA((KB,)),
            pltpu.SemaphoreType.DMA((KB,)),
            pltpu.SemaphoreType.DMA((chunks,)),
            pltpu.SemaphoreType.DMA((blocks, 2)),
            pltpu.SemaphoreType.DMA((blocks, 2)),
            pltpu.SemaphoreType.DMA((blocks, 6)),
            pltpu.SemaphoreType.DMA((blocks, 6)),
        ],
        compiler_params=pltpu.CompilerParams(
            collective_id=0, has_side_effects=True, vmem_limit_bytes=56 * 1024 * 1024
        ),
    )(right_sides, lower_panel, upper_panel)


def solution(mesh):
    placed = (P(("parts", "row"), "col"), P(("parts", "row"), None), P(("parts", "row"), None))
    return jax.shard_map(
        shards, mesh=mesh, in_specs=placed, out_specs=P(("parts", "row"), "col"), check_vma=False
    )
```

```python
import functools

import jax
import jax.numpy as jnp
from jax import lax
from jax.experimental import pallas as pl
from jax.experimental.pallas import tpu as pltpu
from jax.sharding import PartitionSpec as P

NB = 256
KB = 4
CW = 256
HALF = NB // 2
HOP = 2
SLACK = 0


def split(value):
    high = value.astype(jnp.bfloat16)
    low = (value - high.astype(jnp.float32)).astype(jnp.bfloat16)
    return high, low


def mm(a, b):
    return jnp.dot(a, b, preferred_element_type=jnp.float32)


def dot_split(a, b):
    return mm(a[0], b[0]) + (mm(a[0], b[1]) + mm(a[1], b[0]))


def dot3(a, b):
    return dot_split(split(a), split(b))


def triangular_inverses(matrices):
    rows = lax.broadcasted_iota(jnp.int32, (NB, NB), 0)
    columns = lax.broadcasted_iota(jnp.int32, (NB, NB), 1)
    same = rows == columns
    ident = jnp.where(same, 1.0, 0.0).astype(jnp.float32)
    scales, offs = [], []
    for matrix in matrices:
        diagonal = jnp.where(same, matrix, 0.0)
        by_row = 1.0 / jnp.sum(diagonal, axis=1, keepdims=True)
        scales.append(1.0 / jnp.sum(diagonal, axis=0, keepdims=True))
        offs.append(jnp.where(same, 0.0, matrix) * by_row)
    count = range(len(matrices))
    inner = (rows // 16) == (columns // 16)
    powers = [jnp.where(inner, -offs[i], 0.0) for i in count]
    results = [ident + powers[i] for i in count]
    reach = 2
    while reach < 16:
        powers = [dot3(powers[i], powers[i]) for i in count]
        results = [results[i] + dot3(results[i], powers[i]) for i in count]
        reach *= 2
    size = 16
    while size < NB:
        pair = ((rows // (2 * size)) == (columns // (2 * size))) & (
            (rows // size) != (columns // size)
        )
        halves = [split(results[i]) for i in count]
        middle = [
            dot_split(split(jnp.where(pair, offs[i], 0.0)), halves[i]) for i in count
        ]
        results = [results[i] - dot_split(halves[i], split(middle[i])) for i in count]
        size *= 2
    return [results[i] * scales[i] for i in count]


def kernel(
    nx, nz, b_ref, l_ref, u_ref, out_ref,
    acc, xbuf, zbuf, lf, uf, lhi, llo, uhi, ulo, diag, inv_hi, inv_lo,
    b_sem, l_sem, u_sem, d_sem, o_sem, recv_f, recv_b, send_f, send_b,
):
    rows = b_ref.shape[0]
    chunks = b_ref.shape[1] // CW
    blocks = chunks * KB
    n = nx * nz
    me = lax.axis_index("row")
    x = me % nx
    z = me // nx
    is_first = me == 0
    is_last = me == n - 1

    def load_b(c):
        return pltpu.make_async_copy(b_ref.at[:, pl.ds(c * CW, CW)], acc.at[c], b_sem.at[c])

    def load_l(k):
        return pltpu.make_async_copy(l_ref.at[:, pl.ds(k * NB, NB)], lf.at[k], l_sem.at[k])

    def load_u(k):
        return pltpu.make_async_copy(u_ref.at[:, pl.ds(k * NB, NB)], uf.at[k], u_sem.at[k])

    def load_d(source, k):
        return pltpu.make_async_copy(
            source.at[pl.ds(k * NB, NB), pl.ds(k * NB, NB)], diag.at[k], d_sem.at[k]
        )

    def store_out(c):
        return pltpu.make_async_copy(acc.at[c], out_ref.at[:, pl.ds(c * CW, CW)], o_sem.at[c])

    @pl.when(is_first)
    def _():
        for k in range(KB):
            load_d(l_ref, k).start()

    @pl.when(is_last)
    def _():
        for k in range(KB):
            load_d(u_ref, k).start()

    load_b(0).start()
    for k in range(KB):
        load_l(k).start()
    for c in range(1, chunks):
        load_b(c).start()
    for k in range(KB):
        load_u(k).start()

    barrier = pltpu.get_barrier_semaphore()
    neighbours = (
        (x >= 1, me - 1),
        (x < nx - 1, me + 1),
        (z >= 1, me - nx),
        (z < nz - 1, me + nx),
    )
    for there, other in neighbours:
        @pl.when(there)
        def _():
            pl.semaphore_signal(
                barrier, inc=1, device_id={"row": other},
                device_id_type=pl.DeviceIdType.MESH,
            )
    peers = sum(jnp.where(there, 1, 0) for there, _ in neighbours)
    pl.semaphore_wait(barrier, peers)

    @pl.when(is_first | is_last)
    def _():
        for k in range(KB):
            load_d(l_ref, k).wait()
        inverses = triangular_inverses([diag[k] for k in range(KB)])
        for k in range(KB):
            high, low = split(inverses[k])
            inv_hi[k] = high
            inv_lo[k] = low

    def children(px, pz, step):
        along_x, along_z = step, step * nx
        tree_a = (
            ((px == 0) & (pz < nz - 1), me + along_z),
            ((pz >= 1) & (px < nx - 1), me + along_x),
            ((pz == 1) & (px >= 1), me - along_z),
        )
        tree_b = (
            ((pz == 0) & (px < nx - 1), me + along_x),
            ((px >= 1) & (pz < nz - 1), me + along_z),
            ((px == 1) & (pz >= 1), me - along_x),
        )
        return (tree_a, tree_b)

    forward_children = children(x, z, 1)
    backward_children = children(nx - 1 - x, nz - 1 - z, -1)

    def remote(buf, recv, send, block, tree, child, other):
        piece = buf.at[block, pl.ds(tree * HALF, HALF), :]
        return pltpu.make_async_remote_copy(
            src_ref=piece, dst_ref=piece,
            send_sem=send.at[block, tree * 3 + child],
            recv_sem=recv.at[block, tree],
            device_id={"row": other}, device_id_type=pl.DeviceIdType.MESH,
        )

    def pass_on(buf, recv, send, block, tree, kids):
        for child in range(3):
            there, other = kids[tree][child]

            @pl.when(there)
            def _():
                remote(buf, recv, send, block, tree, child, other).start()

    def sent(buf, recv, send, block, kids):
        for tree in range(2):
            for child in range(3):
                there, other = kids[tree][child]

                @pl.when(there)
                def _():
                    remote(buf, recv, send, block, tree, child, other).wait_send()

    def relay(when, recv, send, buf, kids, tree):
        @pl.when((when >= 0) & (when < blocks))
        def _():
            remote(buf, recv, send, when, tree, 0, me).wait_recv()
            pass_on(buf, recv, send, when, tree, kids)

    def sweep_step(block, c, k, owner, buf, recv, send, kids, early, full, high, low, wait_panel):
        @pl.when(owner)
        def _():
            target = acc[c, pl.ds(pl.multiple_of(k * NB, NB), NB), :]
            buf[block] = dot_split((inv_hi[k], inv_lo[k]), split(target))
            for tree in range(2):
                pass_on(buf, recv, send, block, tree, kids)

        @pl.when(early)
        def _():
            wait_panel(k)
            first, second = split(full[k])
            high[k] = first
            low[k] = second

        acc[c] = acc[c] - dot_split((high[k], low[k]), split(buf[block]))

        @pl.when(owner)
        def _():
            acc[c, pl.ds(pl.multiple_of(k * NB, NB), NB), :] = buf[block]

    def depths(px, pz):
        depth_a = jnp.where((pz == 0) & (px >= 1), px + 2, px + pz)
        depth_b = jnp.where((px == 0) & (pz >= 1), pz + 2, px + pz)
        return HOP * depth_a, HOP * depth_b

    fa, fb = depths(x, z)
    ba, bb = depths(nx - 1 - x, nz - 1 - z)
    fc = jnp.maximum(fa, fb)
    bc = jnp.maximum(ba, bb)
    lag = KB - 1 + HOP * (nx + nz - 2) + SLACK
    deepest = HOP * (nx + nz)

    def event(t, carry):
        @pl.when(jnp.logical_not(is_first))
        def _():
            relay(t - fa, recv_f, send_f, xbuf, forward_children, 0)
            relay(t - fb, recv_f, send_f, xbuf, forward_children, 1)

        @pl.when(jnp.logical_not(is_last))
        def _():
            relay(t - lag - ba, recv_b, send_b, zbuf, backward_children, 0)
            relay(t - lag - bb, recv_b, send_b, zbuf, backward_children, 1)

        e = t - fc

        @pl.when((e >= 0) & (e < blocks))
        def _():
            c = e // KB
            k = e % KB

            @pl.when(k == 0)
            def _():
                load_b(c).wait()

            sweep_step(
                e, c, k, is_first, xbuf, recv_f, send_f, forward_children,
                e < KB, lf, lhi, llo, lambda k: load_l(k).wait(),
            )

        j = t - lag - bc

        @pl.when((j >= 0) & (j < blocks))
        def _():
            c = j // KB
            k = KB - 1 - j % KB
            sweep_step(
                j, c, k, is_last, zbuf, recv_b, send_b, backward_children,
                j < KB, uf, uhi, ulo, lambda k: load_u(k).wait(),
            )

            @pl.when(k == 0)
            def _():
                store_out(c).start()

        return carry

    lax.fori_loop(0, blocks + lag + deepest + 1, event, 0)

    def finish(block, carry):
        sent(xbuf, recv_f, send_f, block, forward_children)
        sent(zbuf, recv_b, send_b, block, backward_children)
        return carry

    lax.fori_loop(0, blocks, finish, 0)
    for c in range(chunks):
        store_out(c).wait()


def grid_of(n):
    nx = 2 if n < 32 else 4
    return nx, n // nx


def shards(right_sides, lower_panel, upper_panel):
    rows, width = right_sides.shape
    nx, nz = grid_of(lax.axis_size("row"))
    chunks = width // CW
    blocks = chunks * KB
    f32, bf16 = jnp.float32, jnp.bfloat16
    return pl.pallas_call(
        functools.partial(kernel, nx, nz),
        out_shape=jax.ShapeDtypeStruct((rows, width), f32),
        in_specs=[pl.BlockSpec(memory_space=pl.ANY)] * 3,
        out_specs=pl.BlockSpec(memory_space=pl.ANY),
        scratch_shapes=[
            pltpu.VMEM((chunks, rows, CW), f32),
            pltpu.VMEM((blocks, NB, CW), f32),
            pltpu.VMEM((blocks, NB, CW), f32),
            pltpu.VMEM((KB, rows, NB), f32),
            pltpu.VMEM((KB, rows, NB), f32),
            pltpu.VMEM((KB, rows, NB), bf16),
            pltpu.VMEM((KB, rows, NB), bf16),
            pltpu.VMEM((KB, rows, NB), bf16),
            pltpu.VMEM((KB, rows, NB), bf16),
            pltpu.VMEM((KB, NB, NB), f32),
            pltpu.VMEM((KB, NB, NB), bf16),
            pltpu.VMEM((KB, NB, NB), bf16),
            pltpu.SemaphoreType.DMA((chunks,)),
            pltpu.SemaphoreType.DMA((KB,)),
            pltpu.SemaphoreType.DMA((KB,)),
            pltpu.SemaphoreType.DMA((KB,)),
            pltpu.SemaphoreType.DMA((chunks,)),
            pltpu.SemaphoreType.DMA((blocks, 2)),
            pltpu.SemaphoreType.DMA((blocks, 2)),
            pltpu.SemaphoreType.DMA((blocks, 6)),
            pltpu.SemaphoreType.DMA((blocks, 6)),
        ],
        compiler_params=pltpu.CompilerParams(
            collective_id=0, has_side_effects=True, vmem_limit_bytes=56 * 1024 * 1024
        ),
    )(right_sides, lower_panel, upper_panel)


def solution(mesh):
    placed = (P(("parts", "row"), "col"), P(("parts", "row"), None), P(("parts", "row"), None))
    return jax.shard_map(
        shards, mesh=mesh, in_specs=placed, out_specs=P(("parts", "row"), "col"), check_vma=False
    )
```

```python
import functools

import jax
import jax.numpy as jnp
from jax import lax
from jax.experimental import pallas as pl
from jax.experimental.pallas import tpu as pltpu
from jax.sharding import PartitionSpec as P

NB = 256
KB = 4
CW = 128
HALF = NB // 2
HOP = 2
SLACK = 0


def split(value):
    high = value.astype(jnp.bfloat16)
    low = (value - high.astype(jnp.float32)).astype(jnp.bfloat16)
    return high, low


def mm(a, b):
    return jnp.dot(a, b, preferred_element_type=jnp.float32)


def dot_split(a, b):
    return mm(a[0], b[0]) + (mm(a[0], b[1]) + mm(a[1], b[0]))


def dot3(a, b):
    return dot_split(split(a), split(b))


def triangular_inverses(matrices):
    rows = lax.broadcasted_iota(jnp.int32, (NB, NB), 0)
    columns = lax.broadcasted_iota(jnp.int32, (NB, NB), 1)
    same = rows == columns
    ident = jnp.where(same, 1.0, 0.0).astype(jnp.float32)
    scales, offs = [], []
    for matrix in matrices:
        diagonal = jnp.where(same, matrix, 0.0)
        by_row = 1.0 / jnp.sum(diagonal, axis=1, keepdims=True)
        scales.append(1.0 / jnp.sum(diagonal, axis=0, keepdims=True))
        offs.append(jnp.where(same, 0.0, matrix) * by_row)
    count = range(len(matrices))
    inner = (rows // 16) == (columns // 16)
    powers = [jnp.where(inner, -offs[i], 0.0) for i in count]
    results = [ident + powers[i] for i in count]
    reach = 2
    while reach < 16:
        powers = [dot3(powers[i], powers[i]) for i in count]
        results = [results[i] + dot3(results[i], powers[i]) for i in count]
        reach *= 2
    size = 16
    while size < NB:
        pair = ((rows // (2 * size)) == (columns // (2 * size))) & (
            (rows // size) != (columns // size)
        )
        halves = [split(results[i]) for i in count]
        middle = [
            dot_split(split(jnp.where(pair, offs[i], 0.0)), halves[i]) for i in count
        ]
        results = [results[i] - dot_split(halves[i], split(middle[i])) for i in count]
        size *= 2
    return [results[i] * scales[i] for i in count]


def kernel(
    nx, nz, b_ref, l_ref, u_ref, out_ref,
    acc, xbuf, zbuf, lf, uf, lhi, llo, uhi, ulo, diag, inv_hi, inv_lo,
    b_sem, l_sem, u_sem, d_sem, o_sem, recv_f, recv_b, send_f, send_b,
):
    rows = b_ref.shape[0]
    chunks = b_ref.shape[1] // CW
    blocks = chunks * KB
    n = nx * nz
    me = lax.axis_index("row")
    x = me % nx
    z = me // nx
    is_first = me == 0
    is_last = me == n - 1

    def load_b(c):
        return pltpu.make_async_copy(b_ref.at[:, pl.ds(c * CW, CW)], acc.at[c], b_sem.at[c])

    def load_l(k):
        return pltpu.make_async_copy(l_ref.at[:, pl.ds(k * NB, NB)], lf.at[k], l_sem.at[k])

    def load_u(k):
        return pltpu.make_async_copy(u_ref.at[:, pl.ds(k * NB, NB)], uf.at[k], u_sem.at[k])

    def load_d(source, k):
        return pltpu.make_async_copy(
            source.at[pl.ds(k * NB, NB), pl.ds(k * NB, NB)], diag.at[k], d_sem.at[k]
        )

    def store_out(c):
        return pltpu.make_async_copy(acc.at[c], out_ref.at[:, pl.ds(c * CW, CW)], o_sem.at[c])

    @pl.when(is_first)
    def _():
        for k in range(KB):
            load_d(l_ref, k).start()

    @pl.when(is_last)
    def _():
        for k in range(KB):
            load_d(u_ref, k).start()

    load_b(0).start()
    for k in range(KB):
        load_l(k).start()
    for c in range(1, chunks):
        load_b(c).start()
    for k in range(KB):
        load_u(k).start()

    barrier = pltpu.get_barrier_semaphore()
    neighbours = (
        (x >= 1, me - 1),
        (x < nx - 1, me + 1),
        (z >= 1, me - nx),
        (z < nz - 1, me + nx),
    )
    for there, other in neighbours:
        @pl.when(there)
        def _():
            pl.semaphore_signal(
                barrier, inc=1, device_id={"row": other},
                device_id_type=pl.DeviceIdType.MESH,
            )
    peers = sum(jnp.where(there, 1, 0) for there, _ in neighbours)
    pl.semaphore_wait(barrier, peers)

    @pl.when(is_first | is_last)
    def _():
        for k in range(KB):
            load_d(l_ref, k).wait()
        inverses = triangular_inverses([diag[k] for k in range(KB)])
        for k in range(KB):
            high, low = split(inverses[k])
            inv_hi[k] = high
            inv_lo[k] = low

    def children(px, pz, step):
        along_x, along_z = step, step * nx
        tree_a = (
            ((px == 0) & (pz < nz - 1), me + along_z),
            ((pz >= 1) & (px < nx - 1), me + along_x),
            ((pz == 1) & (px >= 1), me - along_z),
        )
        tree_b = (
            ((pz == 0) & (px < nx - 1), me + along_x),
            ((px >= 1) & (pz < nz - 1), me + along_z),
            ((px == 1) & (pz >= 1), me - along_x),
        )
        return (tree_a, tree_b)

    forward_children = children(x, z, 1)
    backward_children = children(nx - 1 - x, nz - 1 - z, -1)

    def remote(buf, recv, send, block, tree, child, other):
        piece = buf.at[block, pl.ds(tree * HALF, HALF), :]
        return pltpu.make_async_remote_copy(
            src_ref=piece, dst_ref=piece,
            send_sem=send.at[block, tree * 3 + child],
            recv_sem=recv.at[block, tree],
            device_id={"row": other}, device_id_type=pl.DeviceIdType.MESH,
        )

    def pass_on(buf, recv, send, block, tree, kids):
        for child in range(3):
            there, other = kids[tree][child]

            @pl.when(there)
            def _():
                remote(buf, recv, send, block, tree, child, other).start()

    def sent(buf, recv, send, block, kids):
        for tree in range(2):
            for child in range(3):
                there, other = kids[tree][child]

                @pl.when(there)
                def _():
                    remote(buf, recv, send, block, tree, child, other).wait_send()

    def relay(when, recv, send, buf, kids, tree):
        @pl.when((when >= 0) & (when < blocks))
        def _():
            remote(buf, recv, send, when, tree, 0, me).wait_recv()
            pass_on(buf, recv, send, when, tree, kids)

    def sweep_step(block, c, k, owner, buf, recv, send, kids, early, full, high, low, wait_panel):
        @pl.when(owner)
        def _():
            target = acc[c, pl.ds(pl.multiple_of(k * NB, NB), NB), :]
            buf[block] = dot_split((inv_hi[k], inv_lo[k]), split(target))
            for tree in range(2):
                pass_on(buf, recv, send, block, tree, kids)

        @pl.when(early)
        def _():
            wait_panel(k)
            first, second = split(full[k])
            high[k] = first
            low[k] = second

        acc[c] = acc[c] - dot_split((high[k], low[k]), split(buf[block]))

        @pl.when(owner)
        def _():
            acc[c, pl.ds(pl.multiple_of(k * NB, NB), NB), :] = buf[block]

    def depths(px, pz):
        depth_a = jnp.where((pz == 0) & (px >= 1), px + 2, px + pz)
        depth_b = jnp.where((px == 0) & (pz >= 1), pz + 2, px + pz)
        return HOP * depth_a, HOP * depth_b

    fa, fb = depths(x, z)
    ba, bb = depths(nx - 1 - x, nz - 1 - z)
    fc = jnp.maximum(fa, fb)
    bc = jnp.maximum(ba, bb)
    lag = KB - 1 + HOP * (nx + nz - 2) + SLACK
    deepest = HOP * (nx + nz)

    def event(t, carry):
        @pl.when(jnp.logical_not(is_first))
        def _():
            relay(t - fa, recv_f, send_f, xbuf, forward_children, 0)
            relay(t - fb, recv_f, send_f, xbuf, forward_children, 1)

        @pl.when(jnp.logical_not(is_last))
        def _():
            relay(t - lag - ba, recv_b, send_b, zbuf, backward_children, 0)
            relay(t - lag - bb, recv_b, send_b, zbuf, backward_children, 1)

        e = t - fc

        @pl.when((e >= 0) & (e < blocks))
        def _():
            c = e // KB
            k = e % KB

            @pl.when(k == 0)
            def _():
                load_b(c).wait()

            sweep_step(
                e, c, k, is_first, xbuf, recv_f, send_f, forward_children,
                e < KB, lf, lhi, llo, lambda k: load_l(k).wait(),
            )

        j = t - lag - bc

        @pl.when((j >= 0) & (j < blocks))
        def _():
            c = j // KB
            k = KB - 1 - j % KB
            sweep_step(
                j, c, k, is_last, zbuf, recv_b, send_b, backward_children,
                j < KB, uf, uhi, ulo, lambda k: load_u(k).wait(),
            )

            @pl.when(k == 0)
            def _():
                store_out(c).start()

        return carry

    lax.fori_loop(0, blocks + lag + deepest + 1, event, 0)

    def finish(block, carry):
        sent(xbuf, recv_f, send_f, block, forward_children)
        sent(zbuf, recv_b, send_b, block, backward_children)
        return carry

    lax.fori_loop(0, blocks, finish, 0)
    for c in range(chunks):
        store_out(c).wait()


def grid_of(n):
    nx = 2 if n < 32 else 4
    return nx, n // nx


def shards(right_sides, lower_panel, upper_panel):
    rows, width = right_sides.shape
    nx, nz = grid_of(lax.axis_size("row"))
    chunks = width // CW
    blocks = chunks * KB
    f32, bf16 = jnp.float32, jnp.bfloat16
    return pl.pallas_call(
        functools.partial(kernel, nx, nz),
        out_shape=jax.ShapeDtypeStruct((rows, width), f32),
        in_specs=[pl.BlockSpec(memory_space=pl.ANY)] * 3,
        out_specs=pl.BlockSpec(memory_space=pl.ANY),
        scratch_shapes=[
            pltpu.VMEM((chunks, rows, CW), f32),
            pltpu.VMEM((blocks, NB, CW), f32),
            pltpu.VMEM((blocks, NB, CW), f32),
            pltpu.VMEM((KB, rows, NB), f32),
            pltpu.VMEM((KB, rows, NB), f32),
            pltpu.VMEM((KB, rows, NB), bf16),
            pltpu.VMEM((KB, rows, NB), bf16),
            pltpu.VMEM((KB, rows, NB), bf16),
            pltpu.VMEM((KB, rows, NB), bf16),
            pltpu.VMEM((KB, NB, NB), f32),
            pltpu.VMEM((KB, NB, NB), bf16),
            pltpu.VMEM((KB, NB, NB), bf16),
            pltpu.SemaphoreType.DMA((chunks,)),
            pltpu.SemaphoreType.DMA((KB,)),
            pltpu.SemaphoreType.DMA((KB,)),
            pltpu.SemaphoreType.DMA((KB,)),
            pltpu.SemaphoreType.DMA((chunks,)),
            pltpu.SemaphoreType.DMA((blocks, 2)),
            pltpu.SemaphoreType.DMA((blocks, 2)),
            pltpu.SemaphoreType.DMA((blocks, 6)),
            pltpu.SemaphoreType.DMA((blocks, 6)),
        ],
        compiler_params=pltpu.CompilerParams(
            collective_id=0, has_side_effects=True, vmem_limit_bytes=56 * 1024 * 1024
        ),
    )(right_sides, lower_panel, upper_panel)


def solution(mesh):
    placed = (P(("parts", "row"), "col"), P(("parts", "row"), None), P(("parts", "row"), None))
    return jax.shard_map(
        shards, mesh=mesh, in_specs=placed, out_specs=P(("parts", "row"), "col"), check_vma=False
    )
```
